256 devices in a mesh: img: 8 (over y_hi, x), tpl: 32 (over z, y_lo, core).
Axes of the slice: x: 4, y: 4 (y_hi: 2, y_lo: 2; y = y_hi * 2 + y_lo), z: 8, core: 2. Of those that a mesh axis runs over, the one named last changes fastest.
Arguments:
- images: bfloat16 [12288, 2048], P(('img', 'tpl')), may hold values from -320 to 320
- templates: bfloat16 [12288, 2048], P('tpl'), may hold values from -0.62 to 0.62
- class_exponent: int32 [8], replicated, may hold values from 0 to 5
- class_mask: int32 [12288, 8], P('img'), may hold values from 0 to 1, as said below
Outputs:
- new_templates: float32 [12288, 2048], P('tpl', 'img')
- log_evidence: float32 [12288], P('img')
The draws below stay inside these ranges and needn't reach their ends.
Inputs may be any that keep to these rules, and one draw needn't show every extreme that they name: `class_mask`: every image is compared with at least one class.
All inputs are finite; a program needn't handle non-finite values.
Results may differ from the reference program's by a relative error of at most 0.0023.
Values may be sent and summed in bfloat16 or wider, within the bound.
No kernel may reach another device: no remote copies, remote signals or barrier semaphores. Data moves between devices by JAX's collectives and lax.ppermute only.
A program may use at most 64 MiB of HBM per device.

```python
import math
import jax
import jax.numpy as jnp
from jax import lax

F = 2048
CLASSES = 8
IMG_DEV = 1536
IMAGES = 12288
TEMPLATES = 12288
N_IMG = 8


def shared_draw(key):
    key_base = jax.random.fold_in(key, 101)
    key_scale = jax.random.fold_in(key, 102)
    key_pics = jax.random.fold_in(key, 103)
    key_rows = jax.random.fold_in(key, 104)
    base = jnp.clip(jax.random.normal(key_base, (TEMPLATES, F), jnp.float32), -5.0, 5.0)
    tpl_scale = jnp.exp(jax.random.uniform(key_scale, (TEMPLATES, 1), jnp.float32, math.log(0.03), math.log(0.1)))
    pictures = jnp.clip(jax.random.normal(key_pics, (IMAGES, F), jnp.float32), -5.0, 5.0)
    pic_scale = jnp.exp(jax.random.uniform(key_rows, (IMAGES, 1), jnp.float32, math.log(0.5), math.log(2.0)))
    return (base, base * tpl_scale, pictures * pic_scale)


def aligned_draw(base, tmpl, pictures):
    picks = (jnp.arange(8, dtype=jnp.int32) * (TEMPLATES // 8)).astype(jnp.int32)
    rows = base[picks]
    signs = jnp.where(rows >= 0.0, 1.0, -1.0)
    leading = 0.12 * signs * (1.0 + jnp.minimum(jnp.abs(rows), 4.0))
    tmpl = tmpl.at[picks].set(leading).at[picks + 1].set(1.02 * leading)
    targets = (jnp.arange(8, dtype=jnp.int32) * (IMAGES // 8) + 3).astype(jnp.int32)
    factors = jnp.array([6.0, 8.0, 10.0, 12.0, 6.0, 8.0, 10.0, 12.0], jnp.float32)
    norms = jnp.sum(leading * leading, axis=1, keepdims=True)
    gains = 40.0 * factors[:, None] / norms
    pictures = pictures.at[targets].set(gains * leading)
    return (tmpl, pictures)


def draw_images(key, part):
    base, tmpl, pictures = shared_draw(key)
    tmpl, pictures = aligned_draw(base, tmpl, pictures)
    return pictures.astype(jnp.bfloat16)


def draw_templates(key, part):
    base, tmpl, pictures = shared_draw(key)
    tmpl, pictures = aligned_draw(base, tmpl, pictures)
    return tmpl.astype(jnp.bfloat16)


def draw_class_mask(key, part):
    key_bits = jax.random.fold_in(key, 201)
    key_force = jax.random.fold_in(key, 202)
    chosen = jax.random.randint(key_bits, (IMAGES, CLASSES), 0, 4) > 0
    forced = jax.random.randint(key_force, (IMAGES,), 0, CLASSES)
    forced_hit = jnp.arange(CLASSES, dtype=jnp.int32)[None, :] == forced[:, None]
    return jnp.logical_or(chosen, forced_hit).astype(jnp.int32)


def plant(drawn, key, least, high):
    longest = drawn.shape.index(max(drawn.shape))
    spots = []
    for shift in (0, 1):
        where = [jax.random.randint(jax.random.fold_in(key, axis), (), 0, length) for axis, length in enumerate(drawn.shape)]
        where[longest] = (where[longest] + shift) % drawn.shape[longest]
        spots.append(tuple(where))
    return drawn.at[spots[0]].set(least).at[spots[1]].set(high)


def setup_inputs(seed: int = 0) -> dict:
    keys = jax.random.split(jax.random.key(seed), 5)
    return {
        "images": draw_images(jax.random.fold_in(keys[4], 71), 0),
        "templates": draw_templates(jax.random.fold_in(keys[4], 71), 0),
        "class_exponent": plant(jax.random.randint(keys[2], (CLASSES,), 0, 6), jax.random.fold_in(keys[2], 1), 0, 5).astype(jnp.int32),
        "class_mask": draw_class_mask(jax.random.fold_in(keys[4], 71), 0),
    }


floor_score = -1.0e30


def reference(images, templates, class_exponent, class_mask):
    total_rows = templates.shape[0]
    per_class = total_rows // CLASSES
    template_f32 = templates.astype(jnp.float32)
    squared_norm = jnp.sum(template_f32 * template_f32, axis=1)
    owner = (jnp.arange(total_rows, dtype=jnp.int32) // per_class).astype(jnp.int32)
    inverse_temp = 0.5 * jnp.exp2(0.5 * class_exponent.astype(jnp.float32))
    beta = inverse_temp[owner]
    picture_blocks = images.reshape(N_IMG, IMG_DEV, F)
    mask_blocks = class_mask.reshape(N_IMG, IMG_DEV, CLASSES)

    def block_step(carry, item):
        pictures, allow_rows = item
        raw = jnp.dot(pictures, templates.T, preferred_element_type=jnp.float32)
        scores = beta[None, :] * (raw - 0.5 * squared_norm[None, :])
        allowed = allow_rows[:, owner] > 0
        top = jnp.max(jnp.where(allowed, scores, floor_score), axis=1, keepdims=True)
        expo = jnp.where(allowed, jnp.exp(scores - top), 0.0)
        totals = jnp.sum(expo, axis=1, keepdims=True)
        posterior = expo / totals
        weighted = carry[0] + jnp.dot(posterior.astype(jnp.bfloat16).T, pictures, preferred_element_type=jnp.float32)
        occupancy = carry[1] + jnp.sum(posterior, axis=0)
        return (weighted, occupancy), (top + jnp.log(totals))[:, 0]

    start = (jnp.zeros((total_rows, F), jnp.float32), jnp.zeros((total_rows,), jnp.float32))
    (weighted, occupancy), evidence = lax.scan(block_step, start, (picture_blocks, mask_blocks))
    new_templates = (weighted + template_f32) / (occupancy[:, None] + 1.0)
    return new_templates, evidence.reshape(-1)
```

```python
import jax
import jax.numpy as jnp
from jax import lax
from jax.sharding import PartitionSpec as P

f32 = jnp.float32
bf16 = jnp.bfloat16
floor_score = -1e30
Z, Y, C = 8, 2, 2
X = 4


def tpl_perm(step):
    pairs = []
    for z in range(Z):
        for y in range(Y):
            for c in range(C):
                nz, ny, nc = step(z, y, c)
                pairs.append(((z * Y + y) * C + c, ((nz % Z) * Y + ny) * C + nc))
    return pairs


def img_perm(step):
    pairs = []
    for h in range(2):
        for x in range(X):
            nh, nx = step(h, x)
            pairs.append((h * X + x, nh * X + nx % X))
    return pairs


SIBLING = tpl_perm(lambda z, y, c: (z, y, 1 - c))
ACROSS = tpl_perm(lambda z, y, c: (z, 1 - y, c))
RING = tpl_perm(lambda z, y, c: (z + 1 - 2 * c, y, c))


def to_tpl(value, pairs):
    return lax.ppermute(value, "tpl", pairs)


def to_img(value, step):
    return lax.ppermute(value, "img", img_perm(step))


def gather_images(images, z, y, c):
    rows, features = images.shape
    own = images.reshape(1, rows, features)

    def pair(mine):
        other = to_tpl(mine, SIBLING)
        return jnp.where(
            c == 0, jnp.concatenate([mine, other]), jnp.concatenate([other, mine])
        )

    across = to_tpl(own, ACROSS)
    held = [(pair(own), y), (pair(across), 1 - y)]
    parts = [(block, z, row) for block, row in held]
    sign = 1 - 2 * c
    for step in (1, 2, 3):
        moved = []
        for block, row in held:
            block = to_tpl(block, RING)
            moved.append((block, row))
            parts.append((block, z - sign * step, row))
            parts.append((to_tpl(block, SIBLING), z + sign * step, row))
        held = moved
    for block, row in held:
        half = to_tpl(lax.dynamic_slice_in_dim(block, c, 1, 0), RING)
        parts.append((pair(half), z + Z // 2, row))
    gathered = jnp.zeros((Z * Y * C, rows, features), images.dtype)
    for block, at_z, row in parts:
        at = (((at_z + Z) % Z) * Y + row) * C
        gathered = lax.dynamic_update_slice(gathered, block, (at, 0, 0))
    return gathered.reshape(Z * Y * C * rows, features)


def merge(a, b):
    top = jnp.maximum(a[0], b[0])
    total = a[1] * jnp.exp(a[0] - top) + b[1] * jnp.exp(b[0] - top)
    return jnp.stack([top, total])


def per_device(images, templates, class_exponent, class_mask):
    tpl_rows, features = templates.shape
    class_count = class_exponent.shape[0]
    per_class = tpl_rows * lax.axis_size("tpl") // class_count
    t = lax.axis_index("tpl")
    z, y, c = t // (Y * C), (t // C) % Y, t % C
    owner = t * tpl_rows // per_class
    exponent = lax.dynamic_index_in_dim(class_exponent, owner, 0, keepdims=False)
    beta = 0.5 * jnp.exp2(0.5 * exponent.astype(f32))
    allowed = lax.dynamic_index_in_dim(class_mask, owner, 1, keepdims=False) > 0
    half_norm = 0.5 * jnp.sum(jnp.square(templates.astype(f32)), axis=1)

    gathered = gather_images(images, z, y, c)
    raw = lax.dot_general(
        templates, gathered, (((1,), (1,)), ((), ())), preferred_element_type=f32
    )
    scores = beta * (raw - half_norm[:, None])
    local_top = jnp.max(scores, axis=0)
    expo = jnp.exp(scores - local_top[None, :])
    local_total = jnp.sum(expo, axis=0)
    masked_top = jnp.where(allowed, local_top, floor_score)
    stats = jnp.stack([masked_top, jnp.where(allowed, local_total, 0.0)])
    for step in (
        lambda z, y, c: (z, y, 1 - c),
        lambda z, y, c: (z, 1 - y, c),
        lambda z, y, c: (z ^ 1, y, c),
        lambda z, y, c: (z ^ 2, y, c),
        lambda z, y, c: (z ^ 4, y, c),
    ):
        stats = merge(stats, to_tpl(stats, tpl_perm(step)))
    top, totals = stats[0], stats[1]
    factor = jnp.where(allowed, jnp.exp(masked_top - top) / totals, 0.0)
    posterior = expo * factor[None, :]
    posterior_bf = posterior.astype(bf16)

    occupancy = jnp.sum(posterior, axis=1)
    for step in (
        lambda h, x: (h, x ^ 1),
        lambda h, x: (h, x ^ 2),
        lambda h, x: (1 - h, x),
    ):
        occupancy = occupancy + to_img(occupancy, step)

    g = lax.axis_index("img")
    h, x = g // X, g % X
    columns = features // lax.axis_size("img")

    def row_sum(row):
        start = row * X * columns
        side = lax.dynamic_slice_in_dim(gathered, start, X * columns, 1)
        part = lax.dot_general(
            posterior_bf, side, (((1,), (0,)), ((), ())), preferred_element_type=f32
        )

        def block(at):
            return lax.dynamic_slice_in_dim(part, at % X * columns, columns, 1)

        total = block(x)
        for d in (2, 1, 3):
            got = to_img(block(x + d).astype(bf16), lambda hh, xx, d=d: (hh, xx + d))
            total = total + got.astype(f32)
        return total

    far = row_sum(1 - h)
    near = row_sum(h)
    got = to_img(far.astype(bf16), lambda hh, xx: (1 - hh, xx)).astype(f32)
    own_share = near + got
    own_templates = lax.dynamic_slice_in_dim(templates, g * columns, columns, 1)
    new_templates = (own_share + own_templates.astype(f32)) / (occupancy[:, None] + 1.0)
    log_evidence = top + jnp.log(totals)
    return (new_templates, log_evidence)


def solution(mesh):
    in_specs = (P(("img", "tpl"), None), P("tpl", None), P(), P("img", None))
    out_specs = (P("tpl", "img"), P("img"))
    return jax.shard_map(
        per_device, mesh=mesh, in_specs=in_specs, out_specs=out_specs, check_vma=False
    )
```

```python
import jax
import jax.numpy as jnp
from jax import lax
from jax.experimental import pallas as pl
from jax.experimental.pallas import tpu as pltpu
from jax.sharding import PartitionSpec as P

f32 = jnp.float32
bf16 = jnp.bfloat16
floor_score = -1e30
Z, Y, C = 8, 2, 2
X = 4


def tpl_perm(step):
    pairs = []
    for z in range(Z):
        for y in range(Y):
            for c in range(C):
                nz, ny, nc = step(z, y, c)
                pairs.append(((z * Y + y) * C + c, ((nz % Z) * Y + ny) * C + nc))
    return pairs


def img_perm(step):
    pairs = []
    for h in range(2):
        for x in range(X):
            nh, nx = step(h, x)
            pairs.append((h * X + x, nh * X + nx % X))
    return pairs


SIBLING = tpl_perm(lambda z, y, c: (z, y, 1 - c))
ACROSS = tpl_perm(lambda z, y, c: (z, 1 - y, c))
RING = tpl_perm(lambda z, y, c: (z + 1 - 2 * c, y, c))


def to_tpl(value, pairs):
    return lax.ppermute(value, "tpl", pairs)


def to_img(value, step):
    return lax.ppermute(value, "img", img_perm(step))


def gather_images(images, z, y, c):
    rows, features = images.shape
    own = images.reshape(1, rows, features)

    def pair(mine):
        other = to_tpl(mine, SIBLING)
        return jnp.where(
            c == 0, jnp.concatenate([mine, other]), jnp.concatenate([other, mine])
        )

    across = to_tpl(own, ACROSS)
    held = [(pair(own), y), (pair(across), 1 - y)]
    parts = [(block, z, row) for block, row in held]
    sign = 1 - 2 * c
    for step in (1, 2, 3):
        moved = []
        for block, row in held:
            block = to_tpl(block, RING)
            moved.append((block, row))
            parts.append((block, z - sign * step, row))
            parts.append((to_tpl(block, SIBLING), z + sign * step, row))
        held = moved
    for block, row in held:
        half = to_tpl(lax.dynamic_slice_in_dim(block, c, 1, 0), RING)
        parts.append((pair(half), z + Z // 2, row))
    gathered = jnp.zeros((Z * Y * C, rows, features), images.dtype)
    for block, at_z, row in parts:
        at = (((at_z + Z) % Z) * Y + row) * C
        gathered = lax.dynamic_update_slice(gathered, block, (at, 0, 0))
    return gathered.reshape(Z * Y * C * rows, features)


def merge(a, b):
    top = jnp.maximum(a[0], b[0])
    total = a[1] * jnp.exp(a[0] - top) + b[1] * jnp.exp(b[0] - top)
    return jnp.stack([top, total])


EXTRA = 16
vmem = pl.BlockSpec(memory_space=pltpu.VMEM)


def call(kernel, outs, flops, moved, limit=40):
    return pl.pallas_call(
        kernel,
        out_shape=[jax.ShapeDtypeStruct(shape, dtype) for shape, dtype in outs],
        out_specs=[vmem] * len(outs),
        compiler_params=pltpu.CompilerParams(vmem_limit_bytes=limit << 20),
        cost_estimate=pl.CostEstimate(
            flops=flops, bytes_accessed=moved, transcendentals=0
        ),
    )


def eye(rows):
    at = (rows, rows)
    return lax.broadcasted_iota(jnp.int32, at, 0) == lax.broadcasted_iota(jnp.int32, at, 1)


def put_counts(counts, columns):
    rows = []
    for _ in range(3):
        term = counts.astype(bf16).astype(f32)
        counts = counts - term
        at = 0
        while at < term.shape[1]:
            piece = term[:, at : at + columns]
            if piece.shape[1] < columns:
                rest = jnp.zeros((1, columns - piece.shape[1]), f32)
                piece = jnp.concatenate([piece, rest], axis=1)
            rows.append(piece)
            at += columns
    rows.append(jnp.zeros((EXTRA - len(rows), columns), f32))
    return jnp.concatenate(rows, axis=0).astype(bf16)


def get_counts(block, count):
    block = block.astype(f32)
    each = -(-count // block.shape[1])
    total = None
    for term in (2, 1, 0):
        row = jnp.concatenate(
            [block[term * each + i : term * each + i + 1] for i in range(each)], axis=1
        )[:, :count]
        total = row if total is None else total + row
    return total


def send_blocks(p_ref, side_ref, extra, x, out_refs, own_ref):
    rows = p_ref.shape[0]
    columns = own_ref.shape[1]
    for d, out in zip((2, 1, 3, 0), (*out_refs, own_ref)):
        start = pl.multiple_of((x + d) % X * columns, columns)
        part = jnp.dot(
            p_ref[...], side_ref[:, pl.ds(start, columns)], preferred_element_type=f32
        )
        if d:
            out[:rows] = part.astype(bf16)
            out[rows:] = extra
        else:
            out[...] = part


def far_kernel(x_ref, e_ref, c_ref, side_ref, p_ref, m2, m1, m3, own_ref, occ_ref):
    p = e_ref[...] * c_ref[...]
    p_ref[...] = p.astype(bf16)
    rows = p.shape[0]
    counts = jnp.sum(jnp.where(eye(rows), jnp.sum(p, axis=1, keepdims=True), 0.0), axis=0, keepdims=True)
    occ_ref[...] = counts
    extra = put_counts(counts, own_ref.shape[1])
    send_blocks(p_ref, side_ref, extra, x_ref[0], (m2, m1, m3), own_ref)


def near_kernel(x_ref, p_ref, occ_ref, side_ref, m2, m1, m3, own_ref):
    extra = put_counts(occ_ref[...], own_ref.shape[1])
    send_blocks(p_ref, side_ref, extra, x_ref[0], (m2, m1, m3), own_ref)


def added(own_ref, occ_ref, got_refs):
    rows = own_ref.shape[0]
    total, counts = own_ref[...], occ_ref[...]
    for got in got_refs:
        total = total + got[:rows].astype(f32)
        counts = counts + get_counts(got[rows:], rows)
    return total, counts


def across_kernel(own_ref, occ_ref, r2, r1, r3, out_ref):
    rows = own_ref.shape[0]
    total, counts = added(own_ref, occ_ref, (r2, r1, r3))
    out_ref[:rows] = total.astype(bf16)
    out_ref[rows:] = put_counts(counts, own_ref.shape[1])


def last_kernel(own_ref, occ_ref, r2, r1, r3, ry, tpl_ref, out_ref):
    rows = own_ref.shape[0]
    total, counts = added(own_ref, occ_ref, (r2, r1, r3, ry))
    column = jnp.sum(jnp.where(eye(rows), counts, 0.0), axis=1, keepdims=True)
    out_ref[...] = (total + tpl_ref[...].astype(f32)) / (column + 1.0)


def per_device(images, templates, class_exponent, class_mask):
    tpl_rows, features = templates.shape
    class_count = class_exponent.shape[0]
    per_class = tpl_rows * lax.axis_size("tpl") // class_count
    t = lax.axis_index("tpl")
    z, y, c = t // (Y * C), (t // C) % Y, t % C
    owner = t * tpl_rows // per_class
    exponent = lax.dynamic_index_in_dim(class_exponent, owner, 0, keepdims=False)
    beta = 0.5 * jnp.exp2(0.5 * exponent.astype(f32))
    allowed = lax.dynamic_index_in_dim(class_mask, owner, 1, keepdims=False) > 0
    half_norm = 0.5 * jnp.sum(jnp.square(templates.astype(f32)), axis=1)

    gathered = gather_images(images, z, y, c)
    raw = lax.dot_general(
        templates, gathered, (((1,), (1,)), ((), ())), preferred_element_type=f32
    )
    scores = beta * (raw - half_norm[:, None])
    local_top = jnp.max(scores, axis=0)
    expo = jnp.exp(scores - local_top[None, :])
    local_total = jnp.sum(expo, axis=0)
    masked_top = jnp.where(allowed, local_top, floor_score)
    stats = jnp.stack([masked_top, jnp.where(allowed, local_total, 0.0)])
    for step in (
        lambda z, y, c: (z, y, 1 - c),
        lambda z, y, c: (z, 1 - y, c),
        lambda z, y, c: (z ^ 1, y, c),
        lambda z, y, c: (z ^ 2, y, c),
        lambda z, y, c: (z ^ 4, y, c),
    ):
        stats = merge(stats, to_tpl(stats, tpl_perm(step)))
    top, totals = stats[0], stats[1]
    factor = jnp.where(allowed, jnp.exp(masked_top - top) / totals, 0.0)
    g = lax.axis_index("img")
    h, x = g // X, g % X
    columns = features // lax.axis_size("img")
    images_here = gathered.shape[0]
    half = X * columns
    at_x = x.reshape(1)
    message = ((tpl_rows + EXTRA, columns), bf16)
    own = ((tpl_rows, columns), f32)
    flops = 2 * images_here * tpl_rows * half
    scalar = pl.BlockSpec(memory_space=pltpu.SMEM)

    def side(row):
        return lax.dynamic_slice_in_dim(gathered, row * half, half, 1)

    def over_x(parts):
        return [
            to_img(part, lambda hh, xx, d=d: (hh, xx + d))
            for d, part in zip((2, 1, 3), parts)
        ]

    p, f2, f1, f3, far, counts = pl.pallas_call(
        far_kernel,
        in_specs=[scalar, vmem, vmem, vmem],
        out_shape=[
            jax.ShapeDtypeStruct(shape, dtype)
            for shape, dtype in (
                ((tpl_rows, images_here), bf16),
                message,
                message,
                message,
                own,
                ((1, tpl_rows), f32),
            )
        ],
        out_specs=[vmem] * 6,
        compiler_params=pltpu.CompilerParams(vmem_limit_bytes=24 << 20),
        cost_estimate=pl.CostEstimate(
            flops=flops, bytes_accessed=8 << 20, transcendentals=0
        ),
    )(at_x, expo, factor[None, :], side(1 - h))
    got_far = over_x((f2, f1, f3))
    n2, n1, n3, near = pl.pallas_call(
        near_kernel,
        in_specs=[scalar, vmem, vmem, vmem],
        out_shape=[
            jax.ShapeDtypeStruct(shape, dtype)
            for shape, dtype in (message, message, message, own)
        ],
        out_specs=[vmem] * 4,
        compiler_params=pltpu.CompilerParams(vmem_limit_bytes=24 << 20),
        cost_estimate=pl.CostEstimate(
            flops=flops, bytes_accessed=6 << 20, transcendentals=0
        ),
    )(at_x, p, counts, side(h))
    got_near = over_x((n2, n1, n3))
    (out,) = call(across_kernel, [message], 1 << 20, 2 << 20)(far, counts, *got_far)
    got = to_img(out, lambda hh, xx: (1 - hh, xx))
    own_templates = lax.dynamic_slice_in_dim(templates, g * columns, columns, 1)
    (new_templates,) = call(last_kernel, [own], 1 << 20, 2 << 20)(
        near, counts, *got_near, got, own_templates
    )
    log_evidence = top + jnp.log(totals)
    return (new_templates, log_evidence)


def solution(mesh):
    in_specs = (P(("img", "tpl"), None), P("tpl", None), P(), P("img", None))
    out_specs = (P("tpl", "img"), P("img"))
    return jax.shard_map(
        per_device, mesh=mesh, in_specs=in_specs, out_specs=out_specs, check_vma=False
    )
```

```python
import functools

import jax
import jax.numpy as jnp
from jax import lax
from jax.experimental import pallas as pl
from jax.experimental.pallas import tpu as pltpu
from jax.sharding import PartitionSpec as P

f32 = jnp.float32
bf16 = jnp.bfloat16
floor_score = -1e30
Z, Y, C = 8, 2, 2
X = 4


def tpl_perm(step):
    pairs = []
    for z in range(Z):
        for y in range(Y):
            for c in range(C):
                nz, ny, nc = step(z, y, c)
                pairs.append(((z * Y + y) * C + c, ((nz % Z) * Y + ny) * C + nc))
    return pairs


def img_perm(step):
    pairs = []
    for h in range(2):
        for x in range(X):
            nh, nx = step(h, x)
            pairs.append((h * X + x, nh * X + nx % X))
    return pairs


SIBLING = tpl_perm(lambda z, y, c: (z, y, 1 - c))
ACROSS = tpl_perm(lambda z, y, c: (z, 1 - y, c))
RING = tpl_perm(lambda z, y, c: (z + 1 - 2 * c, y, c))


def to_tpl(value, pairs):
    return lax.ppermute(value, "tpl", pairs)


def to_img(value, step):
    return lax.ppermute(value, "img", img_perm(step))


def move_images(images, c):
    def pair(mine):
        other = to_tpl(mine, SIBLING)
        return jnp.where(
            c == 0, jnp.concatenate([mine, other]), jnp.concatenate([other, mine])
        )

    rows = images.shape[0]
    across = to_tpl(images, ACROSS)
    held = [pair(images), pair(across)]
    first = list(held)
    groups = []
    for _ in (1, 2, 3):
        held = [to_tpl(block, RING) for block in held]
        group = []
        for block in held:
            group += [block, to_tpl(block, SIBLING)]
        groups.append(group)
    for block in held:
        half = jnp.where(c == 0, block[:rows], block[rows:])
        first.append(pair(to_tpl(half, RING)))
    return first, groups


def merge(a, b):
    top = jnp.maximum(a[0], b[0])
    total = a[1] * jnp.exp(a[0] - top) + b[1] * jnp.exp(b[0] - top)
    return jnp.stack([top, total])


EXTRA = 16
vmem = pl.BlockSpec(memory_space=pltpu.VMEM)


def call(kernel, operands, outs, flops=0, moved=1 << 20, scalars=0, scratch=(), limit=8):
    smem = pl.BlockSpec(memory_space=pltpu.SMEM)
    return pl.pallas_call(
        kernel,
        in_specs=[smem] * scalars + [vmem] * (len(operands) - scalars),
        out_shape=[jax.ShapeDtypeStruct(shape, dtype) for shape, dtype in outs],
        out_specs=[vmem] * len(outs),
        scratch_shapes=list(scratch),
        compiler_params=pltpu.CompilerParams(vmem_limit_bytes=limit << 20),
        cost_estimate=pl.CostEstimate(
            flops=flops, bytes_accessed=moved, transcendentals=0
        ),
    )(*operands)


def eye(rows):
    at = (rows, rows)
    return lax.broadcasted_iota(jnp.int32, at, 0) == lax.broadcasted_iota(jnp.int32, at, 1)


def put_counts(counts, columns):
    rows = []
    for _ in range(3):
        term = counts.astype(bf16).astype(f32)
        counts = counts - term
        at = 0
        while at < term.shape[1]:
            piece = term[:, at : at + columns]
            if piece.shape[1] < columns:
                rest = jnp.zeros((1, columns - piece.shape[1]), f32)
                piece = jnp.concatenate([piece, rest], axis=1)
            rows.append(piece)
            at += columns
    rows.append(jnp.zeros((EXTRA - len(rows), columns), f32))
    return jnp.concatenate(rows, axis=0).astype(bf16)


def get_counts(block, count):
    block = block.astype(f32)
    each = -(-count // block.shape[1])
    total = None
    for term in (2, 1, 0):
        row = jnp.concatenate(
            [block[term * each + i : term * each + i + 1] for i in range(each)], axis=1
        )[:, :count]
        total = row if total is None else total + row
    return total


def place(t, step):
    z, y, c = t // (Y * C), t // C % Y, t % C
    if step == 0:
        spots = [(z, y), (z, 1 - y), (z + Z // 2, y), (z + Z // 2, 1 - y)]
    else:
        back = (1 - 2 * c) * step
        spots = [(z - back, y), (z + back, y), (z - back, 1 - y), (z + back, 1 - y)]
    return [(at + Z) % Z * Y + row for at, row in spots]


def prepare_kernel(per_owner, t_ref, tpl_ref, mask_ref, norm_ref, rows_ref):
    wide = tpl_ref[...].astype(f32)
    norm_ref[...] = 0.5 * jnp.sum(wide * wide, axis=1, keepdims=True)
    allowed = mask_ref[pl.ds(t_ref[0] // per_owner, 1), :]
    rows_ref[...] = jnp.zeros_like(rows_ref)
    block = allowed.shape[1] // rows_ref.shape[0]
    for i in range(rows_ref.shape[0]):
        rows_ref[i : i + 1, :block] = allowed[:, i * block : (i + 1) * block]


def score_kernel(
    step, per_owner, t_ref, power_ref, mask_ref, norm_ref, tpl_ref, b0, b1, b2, b3, old_ref, e_ref, g_ref, stats_ref
):
    t = t_ref[0]
    blocks = (b0, b1, b2, b3)
    rows = b0.shape[0]
    for i, block in enumerate(blocks):
        g_ref[i * rows : (i + 1) * rows] = block[...]
    raw = lax.dot_general(
        tpl_ref[...], g_ref[...], (((1,), (1,)), ((), ())), preferred_element_type=f32
    )
    power = power_ref[t // per_owner].astype(f32)
    beta = 0.5 * jnp.exp2(0.5 * jnp.full((1, 1), power, f32))
    scores = beta * (raw - norm_ref[...])
    top = jnp.max(scores, axis=0, keepdims=True)
    expo = jnp.exp(scores - top)
    e_ref[...] = expo
    total = jnp.sum(expo, axis=0, keepdims=True)
    stats_ref[...] = old_ref[...]
    for i, at in enumerate(place(t, step)):
        here = slice(i * rows, (i + 1) * rows)
        allowed = mask_ref[pl.ds(at, 1), :rows] > 0
        stats_ref[0, pl.ds(at, 1), :rows] = jnp.where(allowed, top[:, here], floor_score)
        stats_ref[1, pl.ds(at, 1), :rows] = jnp.where(allowed, total[:, here], 0.0)


def send_blocks(p_ref, g_refs, extra, row, x, out_refs, own_ref):
    rows, columns = own_ref.shape
    many = g_refs[0].shape[0]
    for d, out in zip((2, 1, 3, 0), (*out_refs, own_ref)):
        start = pl.multiple_of((row * X + (x + d) % X) * columns, columns)
        part = None
        for i, g in enumerate(g_refs):
            term = jnp.dot(
                p_ref[:, i * many : (i + 1) * many],
                g[:, pl.ds(start, columns)],
                preferred_element_type=f32,
            )
            part = term if part is None else part + term
        if d:
            out[:rows] = part.astype(bf16)
            out[rows:] = extra
        else:
            out[...] = part


def far_kernel(
    t_ref, i_ref, mine_ref, all_ref, e0, e1, e2, e3, g0, g1, g2, g3, p_ref, m2, m1, m3, own_ref, occ_ref, c_ref
):
    t, g = t_ref[0], i_ref[0]
    c_ref[...] = jnp.exp(mine_ref[0] - all_ref[0]) / all_ref[1]
    rows, many = e0.shape
    block = many // 4
    counts = None
    for step, e in enumerate((e0, e1, e2, e3)):
        scale = jnp.concatenate(
            [c_ref[pl.ds(at, 1), :block] for at in place(t, step)], axis=1
        )
        p = e[...] * scale
        p_ref[:, step * many : (step + 1) * many] = p.astype(bf16)
        part = jnp.sum(p, axis=1, keepdims=True)
        counts = part if counts is None else counts + part
    counts = jnp.sum(jnp.where(eye(rows), counts, 0.0), axis=0, keepdims=True)
    occ_ref[...] = counts
    extra = put_counts(counts, own_ref.shape[1])
    send_blocks(p_ref, (g0, g1, g2, g3), extra, 1 - g // X, g % X, (m2, m1, m3), own_ref)


def near_kernel(i_ref, all_ref, p_ref, occ_ref, g0, g1, g2, g3, m2, m1, m3, own_ref, log_ref):
    g = i_ref[0]
    evidence = all_ref[0] + jnp.log(all_ref[1])
    block = log_ref.shape[0] // evidence.shape[0]
    row = jnp.concatenate(
        [evidence[i : i + 1, :block] for i in range(evidence.shape[0])], axis=1
    )
    log_ref[...] = row.reshape(log_ref.shape)
    extra = put_counts(occ_ref[...], own_ref.shape[1])
    send_blocks(p_ref, (g0, g1, g2, g3), extra, g // X, g % X, (m2, m1, m3), own_ref)


def added(own_ref, occ_ref, got_refs):
    rows = own_ref.shape[0]
    total, counts = own_ref[...], occ_ref[...]
    for got in got_refs:
        total = total + got[:rows].astype(f32)
        counts = counts + get_counts(got[rows:], rows)
    return total, counts


def across_kernel(own_ref, occ_ref, r2, r1, r3, out_ref):
    rows = own_ref.shape[0]
    total, counts = added(own_ref, occ_ref, (r2, r1, r3))
    out_ref[:rows] = total.astype(bf16)
    out_ref[rows:] = put_counts(counts, own_ref.shape[1])


def last_kernel(i_ref, own_ref, occ_ref, r2, r1, r3, ry, tpl_ref, out_ref):
    rows, columns = own_ref.shape
    start = pl.multiple_of(i_ref[0] * columns, columns)
    own_templates = tpl_ref[:, pl.ds(start, columns)].astype(f32)
    total, counts = added(own_ref, occ_ref, (r2, r1, r3, ry))
    column = jnp.sum(jnp.where(eye(rows), counts, 0.0), axis=1, keepdims=True)
    out_ref[...] = (total + own_templates) / (column + 1.0)


def per_device(images, templates, class_exponent, class_mask):
    tpl_rows, features = templates.shape
    class_count = class_exponent.shape[0]
    per_class = tpl_rows * lax.axis_size("tpl") // class_count
    per_owner = per_class // tpl_rows
    t = lax.axis_index("tpl")
    g = lax.axis_index("img")
    images, t, g = lax.optimization_barrier((images, t, g))
    at_t, at_g = t.reshape(1), g.reshape(1)

    first, groups = move_images(images, t % C)
    block = first[0].shape[0]
    held = Z * Y
    lanes = 128
    class_mask, templates, groups[0][0] = lax.optimization_barrier(
        (class_mask, templates, groups[0][0])
    )
    half_norm, allowed = call(
        functools.partial(prepare_kernel, per_owner),
        (at_t, templates, class_mask.T),
        [((tpl_rows, 1), f32), ((held, lanes), jnp.int32)],
        1 << 20,
        scalars=1,
    )
    many = 4 * block
    stats = jnp.zeros((2, held, lanes), f32)
    expos, images_of = {}, {}
    for step, group in ((1, groups[0]), (2, groups[1]), (3, groups[2]), (0, first)):
        expos[step], images_of[step], stats = call(
            functools.partial(score_kernel, step, per_owner),
            (at_t, class_exponent, allowed, half_norm, templates, *group, stats),
            [
                ((tpl_rows, many), f32),
                ((many, features), bf16),
                ((2, held, lanes), f32),
            ],
            2 * many * tpl_rows * features,
            6 << 20,
            2,
            limit=8,
        )
    mine = stats
    for step in (
        lambda z, y, c: (z, y, 1 - c),
        lambda z, y, c: (z, 1 - y, c),
        lambda z, y, c: (z ^ 1, y, c),
        lambda z, y, c: (z ^ 2, y, c),
        lambda z, y, c: (z ^ 4, y, c),
    ):
        stats = merge(stats, to_tpl(stats, tpl_perm(step)))

    columns = features // lax.axis_size("img")
    message = ((tpl_rows + EXTRA, columns), bf16)
    own = ((tpl_rows, columns), f32)
    flops = 2 * held * block * tpl_rows * X * columns
    parts = [images_of[i] for i in range(4)]

    def over_x(sent):
        return [
            to_img(part, lambda hh, xx, d=d: (hh, xx + d))
            for d, part in zip((2, 1, 3), sent)
        ]

    p, f2, f1, f3, far, counts = call(
        far_kernel,
        (at_t, at_g, mine, stats, *[expos[i] for i in range(4)], *parts),
        [
            ((tpl_rows, held * block), bf16),
            message,
            message,
            message,
            own,
            ((1, tpl_rows), f32),
        ],
        flops,
        8 << 20,
        2,
        [pltpu.VMEM((held, lanes), f32)],
        limit=16,
    )
    got_far = over_x((f2, f1, f3))
    n2, n1, n3, near, log_evidence = call(
        near_kernel,
        (at_g, stats, p, counts, *parts),
        [message, message, message, own, ((held * block,), f32)],
        flops,
        8 << 20,
        1,
        limit=16,
    )
    got_near = over_x((n2, n1, n3))
    (out,) = call(across_kernel, (far, counts, *got_far), [message])
    got = to_img(out, lambda hh, xx: (1 - hh, xx))
    (new_templates,) = call(
        last_kernel, (at_g, near, counts, *got_near, got, templates), [own], scalars=1
    )
    return (new_templates, log_evidence)


def solution(mesh):
    in_specs = (P(("img", "tpl"), None), P("tpl", None), P(), P("img", None))
    out_specs = (P("tpl", "img"), P("img"))
    return jax.shard_map(
        per_device, mesh=mesh, in_specs=in_specs, out_specs=out_specs, check_vma=False
    )
```

```python
import functools

import jax
import jax.numpy as jnp
from jax import lax
from jax.experimental import pallas as pl
from jax.experimental.pallas import tpu as pltpu
from jax.sharding import PartitionSpec as P

f32 = jnp.float32
bf16 = jnp.bfloat16
floor_score = -1e30
Z, Y, C = 8, 2, 2
X = 4


def tpl_perm(step):
    pairs = []
    for z in range(Z):
        for y in range(Y):
            for c in range(C):
                nz, ny, nc = step(z, y, c)
                pairs.append(((z * Y + y) * C + c, ((nz % Z) * Y + ny) * C + nc))
    return pairs


def img_perm(step):
    pairs = []
    for h in range(2):
        for x in range(X):
            nh, nx = step(h, x)
            pairs.append((h * X + x, nh * X + nx % X))
    return pairs


SIBLING = tpl_perm(lambda z, y, c: (z, y, 1 - c))
ACROSS = tpl_perm(lambda z, y, c: (z, 1 - y, c))
RING = tpl_perm(lambda z, y, c: (z + 1 - 2 * c, y, c))

BACK = tpl_perm(lambda z, y, c: (z - 1 + 2 * c, y, c))
BACK3 = tpl_perm(lambda z, y, c: (z - 3 + 6 * c, y, c))


def to_tpl(value, pairs):
    return lax.ppermute(value, "tpl", pairs)


def to_img(value, step):
    return lax.ppermute(value, "img", img_perm(step))


def after(value, other):
    return lax.optimization_barrier((value, other))[0]


def merge(a, b):
    top = jnp.maximum(a[0], b[0])
    total = a[1] * jnp.exp(a[0] - top) + b[1] * jnp.exp(b[0] - top)
    return jnp.stack([top, total])


EXTRA = 16
vmem = pl.BlockSpec(memory_space=pltpu.VMEM)


def call(kernel, operands, outs, flops=0, moved=1 << 20, scalars=0, scratch=(), limit=8):
    smem = pl.BlockSpec(memory_space=pltpu.SMEM)
    return pl.pallas_call(
        kernel,
        in_specs=[smem] * scalars + [vmem] * (len(operands) - scalars),
        out_shape=[jax.ShapeDtypeStruct(shape, dtype) for shape, dtype in outs],
        out_specs=[vmem] * len(outs),
        scratch_shapes=list(scratch),
        compiler_params=pltpu.CompilerParams(vmem_limit_bytes=limit << 20),
        cost_estimate=pl.CostEstimate(
            flops=flops, bytes_accessed=moved, transcendentals=0
        ),
    )(*operands)


def eye(rows):
    at = (rows, rows)
    return lax.broadcasted_iota(jnp.int32, at, 0) == lax.broadcasted_iota(jnp.int32, at, 1)


def put_counts(counts, columns):
    rows = []
    for _ in range(3):
        term = counts.astype(bf16).astype(f32)
        counts = counts - term
        at = 0
        while at < term.shape[1]:
            piece = term[:, at : at + columns]
            if piece.shape[1] < columns:
                rest = jnp.zeros((1, columns - piece.shape[1]), f32)
                piece = jnp.concatenate([piece, rest], axis=1)
            rows.append(piece)
            at += columns
    rows.append(jnp.zeros((EXTRA - len(rows), columns), f32))
    return jnp.concatenate(rows, axis=0).astype(bf16)


def get_counts(block, count):
    block = block.astype(f32)
    each = -(-count // block.shape[1])
    total = None
    for term in (2, 1, 0):
        row = jnp.concatenate(
            [block[term * each + i : term * each + i + 1] for i in range(each)], axis=1
        )[:, :count]
        total = row if total is None else total + row
    return total


def place(t, step):
    z, y, c = t // (Y * C), t // C % Y, t % C
    if step == 0 or step == Z // 2:
        spots = [(z + step, y), (z + step, 1 - y)]
    else:
        back = (1 - 2 * c) * step
        spots = [(z - back, y), (z + back, y), (z - back, 1 - y), (z + back, 1 - y)]
    return [(at + Z) % Z * Y + row for at, row in spots]


def prepare_kernel(per_owner, t_ref, tpl_ref, mask_ref, norm_ref, rows_ref):
    wide = tpl_ref[...].astype(f32)
    norm_ref[...] = 0.5 * jnp.sum(wide * wide, axis=1, keepdims=True)
    allowed = mask_ref[pl.ds(t_ref[0] // per_owner, 1), :]
    rows_ref[...] = jnp.zeros_like(rows_ref)
    block = allowed.shape[1] // rows_ref.shape[0]
    for i in range(rows_ref.shape[0]):
        rows_ref[i : i + 1, :block] = allowed[:, i * block : (i + 1) * block]


def score_kernel(
    step, per_owner, count, t_ref, power_ref, mask_ref, norm_ref, tpl_ref, *refs
):
    t = t_ref[0]
    blocks = refs[:count]
    old_ref, e_ref, g_ref, stats_ref = refs[count:]
    rows = blocks[0].shape[0]
    for i, block in enumerate(blocks):
        g_ref[i * rows : (i + 1) * rows] = block[...]
    raw = lax.dot_general(
        tpl_ref[...], g_ref[...], (((1,), (1,)), ((), ())), preferred_element_type=f32
    )
    power = power_ref[t // per_owner].astype(f32)
    beta = 0.5 * jnp.exp2(0.5 * jnp.full((1, 1), power, f32))
    scores = beta * (raw - norm_ref[...])
    top = jnp.max(scores, axis=0, keepdims=True)
    expo = jnp.exp(scores - top)
    e_ref[...] = expo
    total = jnp.sum(expo, axis=0, keepdims=True)
    stats_ref[...] = old_ref[...]
    for i, at in enumerate(place(t, step)):
        here = slice(i * rows, (i + 1) * rows)
        allowed = mask_ref[pl.ds(at, 1), :rows] > 0
        stats_ref[0, pl.ds(at, 1), :rows] = jnp.where(allowed, top[:, here], floor_score)
        stats_ref[1, pl.ds(at, 1), :rows] = jnp.where(allowed, total[:, here], 0.0)


def send_blocks(p_ref, g_refs, extra, row, x, out_refs, own_ref):
    rows, columns = own_ref.shape
    for d, out in zip((2, 1, 3, 0), (*out_refs, own_ref)):
        start = pl.multiple_of((row * X + (x + d) % X) * columns, columns)
        part, at = None, 0
        for g in g_refs:
            term = jnp.dot(
                p_ref[:, at : at + g.shape[0]],
                g[:, pl.ds(start, columns)],
                preferred_element_type=f32,
            )
            part = term if part is None else part + term
            at += g.shape[0]
        if d:
            out[:rows] = part.astype(bf16)
            out[rows:] = extra
        else:
            out[...] = part


ORDER = (0, 4, 1, 2, 3)


def far_kernel(t_ref, i_ref, mine_ref, all_ref, *refs):
    e_refs, g_refs = refs[:5], refs[5:10]
    p_ref, m2, m1, m3, own_ref, occ_ref, c_ref = refs[10:]
    t, g = t_ref[0], i_ref[0]
    c_ref[...] = jnp.exp(mine_ref[0] - all_ref[0]) / all_ref[1]
    rows = p_ref.shape[0]
    counts = None
    start = 0
    for step in ORDER:
        e = e_refs[step]
        spots = place(t, step)
        block = e.shape[1] // len(spots)
        scale = jnp.concatenate(
            [c_ref[pl.ds(at, 1), :block] for at in spots], axis=1
        )
        p = e[...] * scale
        p_ref[:, start : start + e.shape[1]] = p.astype(bf16)
        part = jnp.sum(p, axis=1, keepdims=True)
        counts = part if counts is None else counts + part
        start += e.shape[1]
    counts = jnp.sum(jnp.where(eye(rows), counts, 0.0), axis=0, keepdims=True)
    occ_ref[...] = counts
    extra = put_counts(counts, own_ref.shape[1])
    g_refs = [g_refs[step] for step in ORDER]
    send_blocks(p_ref, g_refs, extra, 1 - g // X, g % X, (m2, m1, m3), own_ref)


def near_kernel(i_ref, all_ref, p_ref, occ_ref, *refs):
    g_refs = [refs[step] for step in ORDER]
    m2, m1, m3, own_ref, log_ref = refs[5:]
    g = i_ref[0]
    evidence = all_ref[0] + jnp.log(all_ref[1])
    block = log_ref.shape[0] // evidence.shape[0]
    row = jnp.concatenate(
        [evidence[i : i + 1, :block] for i in range(evidence.shape[0])], axis=1
    )
    log_ref[...] = row.reshape(log_ref.shape)
    extra = put_counts(occ_ref[...], own_ref.shape[1])
    send_blocks(p_ref, g_refs, extra, g // X, g % X, (m2, m1, m3), own_ref)


def added(own_ref, occ_ref, got_refs):
    rows = own_ref.shape[0]
    total, counts = own_ref[...], occ_ref[...]
    for got in got_refs:
        total = total + got[:rows].astype(f32)
        counts = counts + get_counts(got[rows:], rows)
    return total, counts


def across_kernel(own_ref, occ_ref, r2, r1, r3, out_ref):
    rows = own_ref.shape[0]
    total, counts = added(own_ref, occ_ref, (r2, r1, r3))
    out_ref[:rows] = total.astype(bf16)
    out_ref[rows:] = put_counts(counts, own_ref.shape[1])


def last_kernel(i_ref, own_ref, occ_ref, r2, r1, r3, ry, tpl_ref, out_ref):
    rows, columns = own_ref.shape
    start = pl.multiple_of(i_ref[0] * columns, columns)
    own_templates = tpl_ref[:, pl.ds(start, columns)].astype(f32)
    total, counts = added(own_ref, occ_ref, (r2, r1, r3, ry))
    column = jnp.sum(jnp.where(eye(rows), counts, 0.0), axis=1, keepdims=True)
    out_ref[...] = (total + own_templates) / (column + 1.0)


def per_device(images, templates, class_exponent, class_mask):
    tpl_rows, features = templates.shape
    class_count = class_exponent.shape[0]
    per_class = tpl_rows * lax.axis_size("tpl") // class_count
    per_owner = per_class // tpl_rows
    t = lax.axis_index("tpl")
    g = lax.axis_index("img")
    images, t, g = lax.optimization_barrier((images, t, g))
    at_t, at_g = t.reshape(1), g.reshape(1)

    c = t % C
    block = images.shape[0] * C
    held = Z * Y
    lanes = 128

    def pair(one, other):
        return jnp.where(
            c == 0, jnp.concatenate([one, other]), jnp.concatenate([other, one])
        )

    def half_of(pairs):
        return jnp.where(c == 0, pairs[: block // C], pairs[block // C :])

    def ring(value):
        return to_tpl(value, RING)

    def share(value):
        return to_tpl(value, SIBLING)

    def score(step, group, stats):
        many = sum(part.shape[0] for part in group)
        return call(
            functools.partial(score_kernel, step, per_owner, len(group)),
            (at_t, class_exponent, allowed, half_norm, templates, *group, stats),
            [
                ((tpl_rows, many), f32),
                ((many, features), bf16),
                ((2, held, lanes), f32),
            ],
            2 * many * tpl_rows * features,
            6 << 20,
            2,
            limit=8,
        )

    across = to_tpl(images, ACROSS)
    early = ring(images)
    sibling = share(images)
    p0 = pair(images, sibling)
    late = ring(sibling)
    p1 = pair(early, late)
    across = after(across, (p0, early))
    q0 = pair(across, share(across))
    q1 = ring(q0)
    templates, class_mask, _ = lax.optimization_barrier((templates, class_mask, q0))
    half_norm, allowed = call(
        functools.partial(prepare_kernel, per_owner),
        (at_t, templates, class_mask.T),
        [((tpl_rows, 1), f32), ((held, lanes), jnp.int32)],
        1 << 20,
        scalars=1,
    )
    stats = jnp.zeros((2, held, lanes), f32)
    e0, g0, stats = score(0, (p0, q0), stats)
    p1 = after(p1, (q0, half_norm))
    p2 = ring(p1)
    s1 = share(p1)
    q1 = after(q1, stats)
    q2 = ring(q1)
    e1, g1, stats = score(1, (p1, s1, q1, share(q1)), stats)
    p3 = ring(p2)
    s2 = share(p2)
    q2 = after(q2, stats)
    q3 = ring(q2)
    e2, g2, stats = score(2, (p2, s2, q2, share(q2)), stats)
    p4 = ring(half_of(p3))
    s3 = share(p3)
    q3 = after(q3, stats)
    q4 = ring(half_of(q3))
    e3, g3, stats = score(3, (p3, s3, q3, share(q3)), stats)
    p4 = pair(p4, share(p4))
    q4 = after(q4, stats)
    e4, g4, stats = score(4, (p4, pair(q4, share(q4))), stats)
    expos = [e0, e1, e2, e3, e4]
    parts = [g0, g1, g2, g3, g4]
    mine = stats
    stats = merge(stats, share(stats))
    stats = merge(stats, to_tpl(stats, ACROSS))
    got = to_tpl(stats, BACK)
    other = share(got)
    up = jnp.where(c == 0, got, other)
    down = jnp.where(c == 0, other, got)
    two = merge(stats, up)
    three = merge(two, down)
    got = to_tpl(jnp.where(c == 0, three, two), BACK3)
    stats = merge(three, merge(got, share(got)))

    columns = features // lax.axis_size("img")
    message = ((tpl_rows + EXTRA, columns), bf16)
    own = ((tpl_rows, columns), f32)
    flops = 2 * held * block * tpl_rows * X * columns

    def over_x(sent):
        return [
            to_img(part, lambda hh, xx, d=d: (hh, xx + d))
            for d, part in zip((2, 1, 3), sent)
        ]

    p, f2, f1, f3, far, counts = call(
        far_kernel,
        (at_t, at_g, mine, stats, *expos, *parts),
        [
            ((tpl_rows, held * block), bf16),
            message,
            message,
            message,
            own,
            ((1, tpl_rows), f32),
        ],
        flops,
        8 << 20,
        2,
        [pltpu.VMEM((held, lanes), f32)],
        limit=16,
    )
    got_far = over_x((f2, f1, f3))
    n2, n1, n3, near, log_evidence = call(
        near_kernel,
        (at_g, stats, p, counts, *parts),
        [message, message, message, own, ((held * block,), f32)],
        flops,
        8 << 20,
        1,
        limit=16,
    )
    got_near = over_x((n2, n1, n3))
    (out,) = call(across_kernel, (far, counts, *got_far), [message])
    got = to_img(out, lambda hh, xx: (1 - hh, xx))
    (new_templates,) = call(
        last_kernel, (at_g, near, counts, *got_near, got, templates), [own], scalars=1
    )
    return (new_templates, log_evidence)


def solution(mesh):
    in_specs = (P(("img", "tpl"), None), P("tpl", None), P(), P("img", None))
    out_specs = (P("tpl", "img"), P("img"))
    return jax.shard_map(
        per_device, mesh=mesh, in_specs=in_specs, out_specs=out_specs, check_vma=False
    )
```

```python
import functools

import jax
import jax.numpy as jnp
from jax import lax
from jax.experimental import pallas as pl
from jax.experimental.pallas import tpu as pltpu
from jax.sharding import PartitionSpec as P

f32 = jnp.float32
bf16 = jnp.bfloat16
floor_score = -1e30
Z, Y, C = 8, 2, 2
X = 4


def tpl_perm(step):
    pairs = []
    for z in range(Z):
        for y in range(Y):
            for c in range(C):
                nz, ny, nc = step(z, y, c)
                pairs.append(((z * Y + y) * C + c, ((nz % Z) * Y + ny) * C + nc))
    return pairs


def img_perm(step):
    pairs = []
    for h in range(2):
        for x in range(X):
            nh, nx = step(h, x)
            pairs.append((h * X + x, nh * X + nx % X))
    return pairs


SIBLING = tpl_perm(lambda z, y, c: (z, y, 1 - c))
ACROSS = tpl_perm(lambda z, y, c: (z, 1 - y, c))
RING = tpl_perm(lambda z, y, c: (z + 1 - 2 * c, y, c))

BACK = tpl_perm(lambda z, y, c: (z - 1 + 2 * c, y, c))
BACK3 = tpl_perm(lambda z, y, c: (z - 3 + 6 * c, y, c))


def to_tpl(value, pairs):
    return lax.ppermute(value, "tpl", pairs)


def to_img(value, step):
    return lax.ppermute(value, "img", img_perm(step))


def after(value, other):
    return lax.optimization_barrier((value, other))[0]


def merge(a, b):
    top = jnp.maximum(a[0], b[0])
    total = a[1] * jnp.exp(a[0] - top) + b[1] * jnp.exp(b[0] - top)
    return jnp.stack([top, total])


EXTRA = 16
vmem = pl.BlockSpec(memory_space=pltpu.VMEM)


def call(kernel, operands, outs, flops=0, moved=1 << 20, scalars=0, scratch=(), limit=8):
    smem = pl.BlockSpec(memory_space=pltpu.SMEM)
    return pl.pallas_call(
        kernel,
        in_specs=[smem] * scalars + [vmem] * (len(operands) - scalars),
        out_shape=[jax.ShapeDtypeStruct(shape, dtype) for shape, dtype in outs],
        out_specs=[vmem] * len(outs),
        scratch_shapes=list(scratch),
        compiler_params=pltpu.CompilerParams(vmem_limit_bytes=limit << 20),
        cost_estimate=pl.CostEstimate(
            flops=flops, bytes_accessed=moved, transcendentals=0
        ),
    )(*operands)


def eye(rows):
    at = (rows, rows)
    return lax.broadcasted_iota(jnp.int32, at, 0) == lax.broadcasted_iota(jnp.int32, at, 1)


def put_counts(counts, columns):
    rows = []
    for _ in range(3):
        term = counts.astype(bf16).astype(f32)
        counts = counts - term
        at = 0
        while at < term.shape[1]:
            piece = term[:, at : at + columns]
            if piece.shape[1] < columns:
                rest = jnp.zeros((1, columns - piece.shape[1]), f32)
                piece = jnp.concatenate([piece, rest], axis=1)
            rows.append(piece)
            at += columns
    rows.append(jnp.zeros((EXTRA - len(rows), columns), f32))
    return jnp.concatenate(rows, axis=0).astype(bf16)


def get_counts(block, count):
    block = block.astype(f32)
    each = -(-count // block.shape[1])
    total = None
    for term in (2, 1, 0):
        row = jnp.concatenate(
            [block[term * each + i : term * each + i + 1] for i in range(each)], axis=1
        )[:, :count]
        total = row if total is None else total + row
    return total


def place(t, step):
    z, y, c = t // (Y * C), t // C % Y, t % C
    if step == 0 or step == Z // 2:
        spots = [(z + step, y), (z + step, 1 - y)]
    else:
        back = (1 - 2 * c) * step
        spots = [(z - back, y), (z + back, y), (z - back, 1 - y), (z + back, 1 - y)]
    return [(at + Z) % Z * Y + row for at, row in spots]


def prepare_kernel(per_owner, t_ref, tpl_ref, mask_ref, norm_ref, rows_ref):
    wide = tpl_ref[...].astype(f32)
    norm_ref[...] = 0.5 * jnp.sum(wide * wide, axis=1, keepdims=True)
    allowed = mask_ref[pl.ds(t_ref[0] // per_owner, 1), :]
    rows_ref[...] = jnp.zeros_like(rows_ref)
    block = allowed.shape[1] // rows_ref.shape[0]
    for i in range(rows_ref.shape[0]):
        rows_ref[i : i + 1, :block] = allowed[:, i * block : (i + 1) * block]


def score_kernel(
    step, per_owner, count, t_ref, power_ref, mask_ref, norm_ref, tpl_ref, *refs
):
    t = t_ref[0]
    blocks = refs[:count]
    old_ref, e_ref, g_ref, stats_ref = refs[count:]
    rows = blocks[0].shape[0]
    for i, block in enumerate(blocks):
        g_ref[i * rows : (i + 1) * rows] = block[...]
    raw = lax.dot_general(
        tpl_ref[...], g_ref[...], (((1,), (1,)), ((), ())), preferred_element_type=f32
    )
    power = power_ref[t // per_owner].astype(f32)
    beta = 0.5 * jnp.exp2(0.5 * jnp.full((1, 1), power, f32))
    scores = beta * (raw - norm_ref[...])
    top = jnp.max(scores, axis=0, keepdims=True)
    expo = jnp.exp(scores - top)
    e_ref[...] = expo
    total = jnp.sum(expo, axis=0, keepdims=True)
    stats_ref[...] = old_ref[...]
    for i, at in enumerate(place(t, step)):
        here = slice(i * rows, (i + 1) * rows)
        allowed = mask_ref[pl.ds(at, 1), :rows] > 0
        stats_ref[0, pl.ds(at, 1), :rows] = jnp.where(allowed, top[:, here], floor_score)
        stats_ref[1, pl.ds(at, 1), :rows] = jnp.where(allowed, total[:, here], 0.0)


def product(p_ref, g_refs, row, x, d, columns):
    start = pl.multiple_of((row * X + (x + d) % X) * columns, columns)
    part, at = None, 0
    for g in g_refs:
        term = jnp.dot(
            p_ref[:, at : at + g.shape[0]],
            g[:, pl.ds(start, columns)],
            preferred_element_type=f32,
        )
        part = term if part is None else part + term
        at += g.shape[0]
    return part


def fill(out, part, extra):
    rows = part.shape[0]
    out[:rows] = part.astype(bf16)
    out[rows:] = extra


ORDER = (0, 4, 1, 2, 3)


def far_kernel(t_ref, i_ref, mine_ref, all_ref, *refs):
    e_refs, g_refs = refs[:5], refs[5:10]
    p_ref, m2, occ_ref, c_ref = refs[10:]
    t, g = t_ref[0], i_ref[0]
    c_ref[...] = jnp.exp(mine_ref[0] - all_ref[0]) / all_ref[1]
    rows = p_ref.shape[0]
    counts = None
    start = 0
    for step in ORDER:
        e = e_refs[step]
        spots = place(t, step)
        block = e.shape[1] // len(spots)
        scale = jnp.concatenate(
            [c_ref[pl.ds(at, 1), :block] for at in spots], axis=1
        )
        p = e[...] * scale
        p_ref[:, start : start + e.shape[1]] = p.astype(bf16)
        part = jnp.sum(p, axis=1, keepdims=True)
        counts = part if counts is None else counts + part
        start += e.shape[1]
    counts = jnp.sum(jnp.where(eye(rows), counts, 0.0), axis=0, keepdims=True)
    occ_ref[...] = counts
    columns = m2.shape[1]
    part = product(p_ref, [g_refs[step] for step in ORDER], 1 - g // X, g % X, 2, columns)
    fill(m2, part, put_counts(counts, columns))


def beside_kernel(far, i_ref, all_ref, p_ref, occ_ref, *refs):
    g_refs = [refs[step] for step in ORDER]
    m1, m3, own_ref = refs[5:8]
    g = i_ref[0]
    row, x = g // X, g % X
    if far:
        row = 1 - row
    columns = own_ref.shape[1]
    extra = put_counts(occ_ref[...], columns)
    fill(m1, product(p_ref, g_refs, row, x, 1, columns), extra)
    fill(m3, product(p_ref, g_refs, row, x, 3, columns), extra)
    own_ref[...] = product(p_ref, g_refs, row, x, 0, columns)
    if not far:
        log_ref = refs[8]
        evidence = all_ref[0] + jnp.log(all_ref[1])
        block = log_ref.shape[0] // evidence.shape[0]
        wide = jnp.concatenate(
            [evidence[i : i + 1, :block] for i in range(evidence.shape[0])], axis=1
        )
        log_ref[...] = wide.reshape(log_ref.shape)


def joined_kernel(i_ref, p_ref, occ_ref, got_ref, *refs):
    g_refs = [refs[step] for step in ORDER]
    m2 = refs[5]
    g = i_ref[0]
    rows, columns = p_ref.shape[0], m2.shape[1]
    part = product(p_ref, g_refs, g // X, g % X, 2, columns)
    counts = occ_ref[...] + get_counts(got_ref[rows:], rows)
    fill(m2, part + got_ref[:rows].astype(f32), put_counts(counts, columns))


def added(own_ref, occ_ref, got_refs):
    rows = own_ref.shape[0]
    total, counts = own_ref[...], occ_ref[...]
    for got in got_refs:
        total = total + got[:rows].astype(f32)
        counts = counts + get_counts(got[rows:], rows)
    return total, counts


def across_kernel(own_ref, occ_ref, r1, r3, out_ref):
    rows = own_ref.shape[0]
    total, counts = added(own_ref, occ_ref, (r1, r3))
    out_ref[:rows] = total.astype(bf16)
    out_ref[rows:] = put_counts(counts, own_ref.shape[1])


def last_kernel(i_ref, own_ref, occ_ref, r2, r1, r3, ry, tpl_ref, out_ref):
    rows, columns = own_ref.shape
    start = pl.multiple_of(i_ref[0] * columns, columns)
    own_templates = tpl_ref[:, pl.ds(start, columns)].astype(f32)
    total, counts = added(own_ref, occ_ref, (r2, r1, r3, ry))
    column = jnp.sum(jnp.where(eye(rows), counts, 0.0), axis=1, keepdims=True)
    out_ref[...] = (total + own_templates) / (column + 1.0)


def per_device(images, templates, class_exponent, class_mask):
    tpl_rows, features = templates.shape
    class_count = class_exponent.shape[0]
    per_class = tpl_rows * lax.axis_size("tpl") // class_count
    per_owner = per_class // tpl_rows
    t = lax.axis_index("tpl")
    g = lax.axis_index("img")
    images, t, g = lax.optimization_barrier((images, t, g))
    at_t, at_g = t.reshape(1), g.reshape(1)

    c = t % C
    block = images.shape[0] * C
    held = Z * Y
    lanes = 128

    def pair(one, other):
        return jnp.where(
            c == 0, jnp.concatenate([one, other]), jnp.concatenate([other, one])
        )

    def half_of(pairs):
        return jnp.where(c == 0, pairs[: block // C], pairs[block // C :])

    def ring(value):
        return to_tpl(value, RING)

    def share(value):
        return to_tpl(value, SIBLING)

    def score(step, group, stats):
        many = sum(part.shape[0] for part in group)
        return call(
            functools.partial(score_kernel, step, per_owner, len(group)),
            (at_t, class_exponent, allowed, half_norm, templates, *group, stats),
            [
                ((tpl_rows, many), f32),
                ((many, features), bf16),
                ((2, held, lanes), f32),
            ],
            2 * many * tpl_rows * features,
            6 << 20,
            2,
            limit=8,
        )

    across = to_tpl(images, ACROSS)
    early = ring(images)
    sibling = share(images)
    p0 = pair(images, sibling)
    late = ring(sibling)
    p1 = pair(early, late)
    across = after(across, (p0, early))
    q0 = pair(across, share(across))
    q1 = ring(q0)
    templates, class_mask, _ = lax.optimization_barrier((templates, class_mask, q0))
    half_norm, allowed = call(
        functools.partial(prepare_kernel, per_owner),
        (at_t, templates, class_mask.T),
        [((tpl_rows, 1), f32), ((held, lanes), jnp.int32)],
        1 << 20,
        scalars=1,
    )
    stats = jnp.zeros((2, held, lanes), f32)
    e0, g0, stats = score(0, (p0, q0), stats)
    p1 = after(p1, (q0, half_norm))
    p2 = ring(p1)
    s1 = share(p1)
    q1 = after(q1, stats)
    q2 = ring(q1)
    e1, g1, stats = score(1, (p1, s1, q1, share(q1)), stats)
    p3 = ring(p2)
    s2 = share(p2)
    q2 = after(q2, stats)
    q3 = ring(q2)
    e2, g2, stats = score(2, (p2, s2, q2, share(q2)), stats)
    p4 = ring(half_of(p3))
    s3 = share(p3)
    q3 = after(q3, stats)
    q4 = ring(half_of(q3))
    e3, g3, stats = score(3, (p3, s3, q3, share(q3)), stats)
    p4 = pair(p4, share(p4))
    q4 = after(q4, stats)
    e4, g4, stats = score(4, (p4, pair(q4, share(q4))), stats)
    expos = [e0, e1, e2, e3, e4]
    parts = [g0, g1, g2, g3, g4]
    mine = stats
    stats = merge(stats, share(stats))
    stats = merge(stats, to_tpl(stats, ACROSS))
    got = to_tpl(stats, BACK)
    other = share(got)
    up = jnp.where(c == 0, got, other)
    down = jnp.where(c == 0, other, got)
    two = merge(stats, up)
    three = merge(two, down)
    got = to_tpl(jnp.where(c == 0, three, two), BACK3)
    stats = merge(three, merge(got, share(got)))

    columns = features // lax.axis_size("img")
    message = ((tpl_rows + EXTRA, columns), bf16)
    own = ((tpl_rows, columns), f32)
    flops = 2 * held * block * tpl_rows * X * columns

    def over_x(part, d):
        return to_img(part, lambda hh, xx: (hh, xx + d))

    def over_y(part):
        return to_img(part, lambda hh, xx: (1 - hh, xx))

    p, f2, counts = call(
        far_kernel,
        (at_t, at_g, mine, stats, *expos, *parts),
        [((tpl_rows, held * block), bf16), message, ((1, tpl_rows), f32)],
        flops // 4,
        4 << 20,
        2,
        [pltpu.VMEM((held, lanes), f32)],
        limit=16,
    )
    far2 = over_y(f2)
    f1, f3, far = call(
        functools.partial(beside_kernel, True),
        (at_g, stats, p, counts, *parts),
        [message, message, own],
        flops,
        6 << 20,
        1,
        limit=16,
    )
    far1, far3 = over_x(f1, 1), over_x(f3, 3)
    counts_near = after(counts, (f1, f3))
    n1, n3, near, log_evidence = call(
        functools.partial(beside_kernel, False),
        (at_g, stats, p, counts_near, *parts),
        [message, message, own, ((held * block,), f32)],
        flops,
        6 << 20,
        1,
        limit=16,
    )
    near1, near3 = over_x(n1, 1), over_x(n3, 3)
    (n2,) = call(
        joined_kernel,
        (at_g, p, counts, after(far2, (n1, n3)), *parts),
        [message],
        flops // 4,
        4 << 20,
        1,
        limit=16,
    )
    got_near = [over_x(n2, 2), near1, near3]
    (out,) = call(across_kernel, (far, counts, far1, far3), [message])
    got = over_y(out)
    (new_templates,) = call(
        last_kernel, (at_g, near, counts, *got_near, got, templates), [own], scalars=1
    )
    return (new_templates, log_evidence)


def solution(mesh):
    in_specs = (P(("img", "tpl"), None), P("tpl", None), P(), P("img", None))
    out_specs = (P("tpl", "img"), P("img"))
    return jax.shard_map(
        per_device, mesh=mesh, in_specs=in_specs, out_specs=out_specs, check_vma=False
    )
```

```python
import functools

import jax
import jax.numpy as jnp
from jax import lax
from jax.experimental import pallas as pl
from jax.experimental.pallas import tpu as pltpu
from jax.sharding import PartitionSpec as P

f32 = jnp.float32
bf16 = jnp.bfloat16
floor_score = -1e30
Z, Y, C = 8, 2, 2
X = 4


def tpl_perm(step):
    pairs = []
    for z in range(Z):
        for y in range(Y):
            for c in range(C):
                nz, ny, nc = step(z, y, c)
                pairs.append(((z * Y + y) * C + c, ((nz % Z) * Y + ny) * C + nc))
    return pairs


def img_perm(step):
    pairs = []
    for h in range(2):
        for x in range(X):
            nh, nx = step(h, x)
            pairs.append((h * X + x, nh * X + nx % X))
    return pairs


SIBLING = tpl_perm(lambda z, y, c: (z, y, 1 - c))
ACROSS = tpl_perm(lambda z, y, c: (z, 1 - y, c))
RING = tpl_perm(lambda z, y, c: (z + 1 - 2 * c, y, c))

BACK = tpl_perm(lambda z, y, c: (z - 1 + 2 * c, y, c))
BACK3 = tpl_perm(lambda z, y, c: (z - 3 + 6 * c, y, c))


def to_tpl(value, pairs):
    return lax.ppermute(value, "tpl", pairs)


def to_img(value, step):
    return lax.ppermute(value, "img", img_perm(step))


def after(value, other):
    return lax.optimization_barrier((value, other))[0]


def merge(a, b):
    top = jnp.maximum(a[0], b[0])
    total = a[1] * jnp.exp(a[0] - top) + b[1] * jnp.exp(b[0] - top)
    return jnp.stack([top, total])


EXTRA = 16
vmem = pl.BlockSpec(memory_space=pltpu.VMEM)


def call(kernel, operands, outs, flops=0, moved=1 << 20, scalars=0, scratch=(), limit=8):
    smem = pl.BlockSpec(memory_space=pltpu.SMEM)
    return pl.pallas_call(
        kernel,
        in_specs=[smem] * scalars + [vmem] * (len(operands) - scalars),
        out_shape=[jax.ShapeDtypeStruct(shape, dtype) for shape, dtype in outs],
        out_specs=[vmem] * len(outs),
        scratch_shapes=list(scratch),
        compiler_params=pltpu.CompilerParams(vmem_limit_bytes=limit << 20),
        cost_estimate=pl.CostEstimate(
            flops=flops, bytes_accessed=moved, transcendentals=0
        ),
    )(*operands)


def eye(rows):
    at = (rows, rows)
    return lax.broadcasted_iota(jnp.int32, at, 0) == lax.broadcasted_iota(jnp.int32, at, 1)


def put_counts(counts, columns):
    rows = []
    for _ in range(3):
        term = counts.astype(bf16).astype(f32)
        counts = counts - term
        at = 0
        while at < term.shape[1]:
            piece = term[:, at : at + columns]
            if piece.shape[1] < columns:
                rest = jnp.zeros((1, columns - piece.shape[1]), f32)
                piece = jnp.concatenate([piece, rest], axis=1)
            rows.append(piece)
            at += columns
    rows.append(jnp.zeros((EXTRA - len(rows), columns), f32))
    return jnp.concatenate(rows, axis=0).astype(bf16)


def get_counts(block, count):
    block = block.astype(f32)
    each = -(-count // block.shape[1])
    total = None
    for term in (2, 1, 0):
        row = jnp.concatenate(
            [block[term * each + i : term * each + i + 1] for i in range(each)], axis=1
        )[:, :count]
        total = row if total is None else total + row
    return total


def place(t, step):
    z, y, c = t // (Y * C), t // C % Y, t % C
    if step == 0 or step == Z // 2:
        spots = [(z + step, y), (z + step, 1 - y)]
    else:
        back = (1 - 2 * c) * step
        spots = [(z - back, y), (z + back, y), (z - back, 1 - y), (z + back, 1 - y)]
    return [(at + Z) % Z * Y + row for at, row in spots]


def prepare_kernel(per_owner, t_ref, tpl_ref, mask_ref, norm_ref, rows_ref):
    wide = tpl_ref[...].astype(f32)
    norm_ref[...] = 0.5 * jnp.sum(wide * wide, axis=1, keepdims=True)
    allowed = mask_ref[pl.ds(t_ref[0] // per_owner, 1), :]
    rows_ref[...] = jnp.zeros_like(rows_ref)
    block = allowed.shape[1] // rows_ref.shape[0]
    for i in range(rows_ref.shape[0]):
        rows_ref[i : i + 1, :block] = allowed[:, i * block : (i + 1) * block]


def score_kernel(
    step, per_owner, count, t_ref, power_ref, mask_ref, norm_ref, tpl_ref, *refs
):
    t = t_ref[0]
    blocks = refs[:count]
    old_ref, e_ref, g_ref, stats_ref = refs[count:]
    rows = blocks[0].shape[0]
    for i, block in enumerate(blocks):
        g_ref[i * rows : (i + 1) * rows] = block[...]
    raw = lax.dot_general(
        tpl_ref[...], g_ref[...], (((1,), (1,)), ((), ())), preferred_element_type=f32
    )
    power = power_ref[t // per_owner].astype(f32)
    beta = 0.5 * jnp.exp2(0.5 * jnp.full((1, 1), power, f32))
    scores = beta * (raw - norm_ref[...])
    top = jnp.max(scores, axis=0, keepdims=True)
    expo = jnp.exp(scores - top)
    e_ref[...] = expo
    total = jnp.sum(expo, axis=0, keepdims=True)
    stats_ref[...] = old_ref[...]
    for i, at in enumerate(place(t, step)):
        here = slice(i * rows, (i + 1) * rows)
        allowed = mask_ref[pl.ds(at, 1), :rows] > 0
        stats_ref[0, pl.ds(at, 1), :rows] = jnp.where(allowed, top[:, here], floor_score)
        stats_ref[1, pl.ds(at, 1), :rows] = jnp.where(allowed, total[:, here], 0.0)


def product(p_ref, g_refs, row, x, d, columns):
    start = pl.multiple_of((row * X + (x + d) % X) * columns, columns)
    part, at = None, 0
    for g in g_refs:
        term = jnp.dot(
            p_ref[:, at : at + g.shape[0]],
            g[:, pl.ds(start, columns)],
            preferred_element_type=f32,
        )
        part = term if part is None else part + term
        at += g.shape[0]
    return part


def fill(out, part, extra):
    rows = part.shape[0]
    out[:rows] = part.astype(bf16)
    out[rows:] = extra


ORDER = (0, 4, 1, 2, 3)


def far_kernel(t_ref, i_ref, mine_ref, all_ref, *refs):
    e_refs, g_refs = refs[:5], refs[5:10]
    p_ref, m1, m3, occ_ref, c_ref = refs[10:]
    t, g = t_ref[0], i_ref[0]
    c_ref[...] = jnp.exp(mine_ref[0] - all_ref[0]) / all_ref[1]
    rows = p_ref.shape[0]
    counts = None
    start = 0
    for step in ORDER:
        e = e_refs[step]
        spots = place(t, step)
        block = e.shape[1] // len(spots)
        scale = jnp.concatenate(
            [c_ref[pl.ds(at, 1), :block] for at in spots], axis=1
        )
        p = e[...] * scale
        p_ref[:, start : start + e.shape[1]] = p.astype(bf16)
        part = jnp.sum(p, axis=1, keepdims=True)
        counts = part if counts is None else counts + part
        start += e.shape[1]
    counts = jnp.sum(jnp.where(eye(rows), counts, 0.0), axis=0, keepdims=True)
    occ_ref[...] = counts
    columns = m1.shape[1]
    extra = put_counts(counts, columns)
    g_refs = [g_refs[step] for step in ORDER]
    for d, out in ((1, m1), (3, m3)):
        fill(out, product(p_ref, g_refs, 1 - g // X, g % X, d, columns), extra)


def rest_kernel(i_ref, p_ref, occ_ref, *refs):
    g_refs = [refs[step] for step in ORDER]
    m2, own_ref = refs[5:]
    g = i_ref[0]
    row, x, columns = 1 - g // X, g % X, own_ref.shape[1]
    part = product(p_ref, g_refs, row, x, 2, columns)
    fill(m2, part, put_counts(occ_ref[...], columns))
    own_ref[...] = product(p_ref, g_refs, row, x, 0, columns)


def beside_kernel(i_ref, p_ref, occ_ref, *refs):
    g_refs = [refs[step] for step in ORDER]
    g = i_ref[0]
    columns = refs[5].shape[1]
    extra = put_counts(occ_ref[...], columns)
    for d, out in ((1, refs[5]), (3, refs[6])):
        fill(out, product(p_ref, g_refs, g // X, g % X, d, columns), extra)


def own_kernel(i_ref, all_ref, p_ref, *refs):
    g_refs = [refs[step] for step in ORDER]
    own_ref, log_ref = refs[5:]
    g = i_ref[0]
    own_ref[...] = product(p_ref, g_refs, g // X, g % X, 0, own_ref.shape[1])
    evidence = all_ref[0] + jnp.log(all_ref[1])
    block = log_ref.shape[0] // evidence.shape[0]
    wide = jnp.concatenate(
        [evidence[i : i + 1, :block] for i in range(evidence.shape[0])], axis=1
    )
    log_ref[...] = wide.reshape(log_ref.shape)


def joined_kernel(i_ref, p_ref, occ_ref, got_ref, *refs):
    g_refs = [refs[step] for step in ORDER]
    m2 = refs[5]
    g = i_ref[0]
    rows, columns = p_ref.shape[0], m2.shape[1]
    part = product(p_ref, g_refs, g // X, g % X, 2, columns)
    counts = occ_ref[...] + get_counts(got_ref[rows:], rows)
    fill(m2, part + got_ref[:rows].astype(f32), put_counts(counts, columns))


def added(own_ref, occ_ref, got_refs):
    rows = own_ref.shape[0]
    total, counts = own_ref[...], occ_ref[...]
    for got in got_refs:
        total = total + got[:rows].astype(f32)
        counts = counts + get_counts(got[rows:], rows)
    return total, counts


def across_kernel(own_ref, occ_ref, r1, r3, out_ref):
    rows = own_ref.shape[0]
    total, counts = added(own_ref, occ_ref, (r1, r3))
    out_ref[:rows] = total.astype(bf16)
    out_ref[rows:] = put_counts(counts, own_ref.shape[1])


def last_kernel(i_ref, own_ref, occ_ref, r2, r1, r3, ry, tpl_ref, out_ref):
    rows, columns = own_ref.shape
    start = pl.multiple_of(i_ref[0] * columns, columns)
    own_templates = tpl_ref[:, pl.ds(start, columns)].astype(f32)
    total, counts = added(own_ref, occ_ref, (r2, r1, r3, ry))
    column = jnp.sum(jnp.where(eye(rows), counts, 0.0), axis=1, keepdims=True)
    out_ref[...] = (total + own_templates) / (column + 1.0)


def per_device(images, templates, class_exponent, class_mask):
    tpl_rows, features = templates.shape
    class_count = class_exponent.shape[0]
    per_class = tpl_rows * lax.axis_size("tpl") // class_count
    per_owner = per_class // tpl_rows
    t = lax.axis_index("tpl")
    g = lax.axis_index("img")
    images, t, g = lax.optimization_barrier((images, t, g))
    at_t, at_g = t.reshape(1), g.reshape(1)

    c = t % C
    block = images.shape[0] * C
    held = Z * Y
    lanes = 128

    def pair(one, other):
        return jnp.where(
            c == 0, jnp.concatenate([one, other]), jnp.concatenate([other, one])
        )

    def half_of(pairs):
        return jnp.where(c == 0, pairs[: block // C], pairs[block // C :])

    def ring(value):
        return to_tpl(value, RING)

    def share(value):
        return to_tpl(value, SIBLING)

    def score(step, group, stats):
        many = sum(part.shape[0] for part in group)
        return call(
            functools.partial(score_kernel, step, per_owner, len(group)),
            (at_t, class_exponent, allowed, half_norm, templates, *group, stats),
            [
                ((tpl_rows, many), f32),
                ((many, features), bf16),
                ((2, held, lanes), f32),
            ],
            2 * many * tpl_rows * features,
            6 << 20,
            2,
            limit=8,
        )

    across = to_tpl(images, ACROSS)
    early = ring(images)
    sibling = share(images)
    p0 = pair(images, sibling)
    late = ring(sibling)
    p1 = pair(early, late)
    across = after(across, (p0, early))
    q0 = pair(across, share(across))
    q1 = ring(q0)
    templates, class_mask, _ = lax.optimization_barrier((templates, class_mask, q0))
    half_norm, allowed = call(
        functools.partial(prepare_kernel, per_owner),
        (at_t, templates, class_mask.T),
        [((tpl_rows, 1), f32), ((held, lanes), jnp.int32)],
        1 << 20,
        scalars=1,
    )
    stats = jnp.zeros((2, held, lanes), f32)
    e0, g0, stats = score(0, (p0, q0), stats)
    p1 = after(p1, (q0, half_norm))
    p2 = ring(p1)
    s1 = share(p1)
    q1 = after(q1, stats)
    q2 = ring(q1)
    e1, g1, stats = score(1, (p1, s1, q1, share(q1)), stats)
    p3 = ring(p2)
    s2 = share(p2)
    q2 = after(q2, stats)
    q3 = ring(q2)
    e2, g2, stats = score(2, (p2, s2, q2, share(q2)), stats)
    p4 = ring(half_of(p3))
    s3 = share(p3)
    q3 = after(q3, stats)
    q4 = ring(half_of(q3))
    e3, g3, stats = score(3, (p3, s3, q3, share(q3)), stats)
    p4 = pair(p4, share(p4))
    q4 = after(q4, stats)
    e4, g4, stats = score(4, (p4, pair(q4, share(q4))), stats)
    expos = [e0, e1, e2, e3, e4]
    parts = [g0, g1, g2, g3, g4]
    mine = stats
    stats = merge(stats, share(stats))
    stats = merge(stats, to_tpl(stats, ACROSS))
    got = to_tpl(stats, BACK)
    other = share(got)
    up = jnp.where(c == 0, got, other)
    down = jnp.where(c == 0, other, got)
    two = merge(stats, up)
    three = merge(two, down)
    got = to_tpl(jnp.where(c == 0, three, two), BACK3)
    stats = merge(three, merge(got, share(got)))

    columns = features // lax.axis_size("img")
    message = ((tpl_rows + EXTRA, columns), bf16)
    own = ((tpl_rows, columns), f32)
    flops = 2 * held * block * tpl_rows * X * columns

    def over_x(part, d):
        return to_img(part, lambda hh, xx: (hh, xx + d))

    def over_y(part):
        return to_img(part, lambda hh, xx: (1 - hh, xx))

    p, f1, f3, counts = call(
        far_kernel,
        (at_t, at_g, mine, stats, *expos, *parts),
        [((tpl_rows, held * block), bf16), message, message, ((1, tpl_rows), f32)],
        flops // 4,
        4 << 20,
        2,
        [pltpu.VMEM((held, lanes), f32)],
        limit=16,
    )
    far1, far3 = over_x(f1, 1), over_x(f3, 3)
    f2, far = call(
        rest_kernel,
        (at_g, p, counts, *parts),
        [message, own],
        flops // 2,
        6 << 20,
        1,
        limit=16,
    )
    far2 = over_y(f2)
    counts_near = after(counts, f2)
    n1, n3 = call(
        beside_kernel,
        (at_g, p, counts_near, *parts),
        [message, message],
        flops // 2,
        6 << 20,
        1,
        limit=16,
    )
    near1, near3 = over_x(n1, 1), over_x(n3, 3)
    (n2,) = call(
        joined_kernel,
        (at_g, p, counts, after(far2, (n1, n3)), *parts),
        [message],
        flops // 4,
        4 << 20,
        1,
        limit=16,
    )
    got_near = [over_x(n2, 2), near1, near3]
    near, log_evidence = call(
        own_kernel,
        (at_g, after(stats, n2), p, *parts),
        [own, ((held * block,), f32)],
        flops // 4,
        4 << 20,
        1,
        limit=16,
    )
    (out,) = call(across_kernel, (far, counts, far1, far3), [message])
    got = over_y(out)
    (new_templates,) = call(
        last_kernel, (at_g, near, counts, *got_near, got, templates), [own], scalars=1
    )
    return (new_templates, log_evidence)


def solution(mesh):
    in_specs = (P(("img", "tpl"), None), P("tpl", None), P(), P("img", None))
    out_specs = (P("tpl", "img"), P("img"))
    return jax.shard_map(
        per_device, mesh=mesh, in_specs=in_specs, out_specs=out_specs, check_vma=False
    )
```
